256 devices in a mesh: dp: 2 (over y_hi), mx: 16 (over x, y_lo, core), my: 8 (over z).
Axes of the slice: x: 4, y: 4 (y_hi: 2, y_lo: 2; y = y_hi * 2 + y_lo), z: 8, core: 2. Of those that a mesh axis runs over, the one named last changes fastest.
Arguments:
- normed_input: bfloat16 [2048, 6144], P('dp', 'mx'), may hold values from -6 to 6
- out_grad: bfloat16 [2048, 6144], P('dp', 'mx'), may hold values from -6 to 6
- w_in: bfloat16 [6144, 24576], P('mx', 'my'), may hold values from -0.078125 to 0.078125
- w_out: bfloat16 [24576, 6144], P('my', 'mx'), may hold values from -0.0390625 to 0.0390625
Outputs:
- in_grad: bfloat16 [2048, 6144], P(('dp', 'my'), 'mx')
- grad_w_in: bfloat16 [6144, 24576], P('mx', 'my')
- grad_w_out: bfloat16 [24576, 6144], P('my', 'mx')
The draws below stay inside these ranges and needn't reach their ends.
All inputs are finite; a program needn't handle non-finite values.
Results may differ from the reference program's by a relative error of at most 0.03.
Values may be sent and summed in bfloat16 or wider, within the bound.
A program may use at most 128 MiB of HBM per device.

```python
import math
import jax
import jax.numpy as jnp
from jax import lax

D = 6144
FF = 24576
TOK_DEV = 1024
TOKENS = 2048
N_DP = 2
N_MX = 16


def shard_levels(rng, shape, split, least, largest):
    factor_of, own = 1.0, jax.random.fold_in(rng, 6)
    for position, shards_of in split:
        steps = jnp.exp(jax.random.uniform(jax.random.fold_in(own, position), (shards_of,), jnp.float32, least / len(split), largest / len(split)))
        factor_of = factor_of * jnp.repeat(steps, shape[position] // shards_of).reshape([-1 if axis == position else 1 for axis in range(len(shape))])
    return factor_of


def centred(rng, shape, scale, limit, split=(), kind=jnp.bfloat16):
    gain = shard_levels(rng, shape, split, -0.22, 0.18) if split else 1.0
    entries = jax.random.normal(rng, shape, jnp.float32) * scale * gain
    return jnp.minimum(jnp.maximum(entries, -limit), limit).astype(kind)


def setup_inputs(seed: int = 0) -> dict:
    seeds = jax.random.split(jax.random.key(seed), 5)
    normed_input = centred(seeds[0], (TOKENS, D), 1.0, 6.0, ((0, 2), (1, 16)))
    out_grad = centred(seeds[1], (TOKENS, D), 1.0, 6.0, ((0, 2), (1, 16)))
    w_in = centred(seeds[2], (D, FF), D ** -0.5, 0.078125, ((0, 16), (1, 8)))
    w_out = centred(seeds[3], (FF, D), FF ** -0.5, 0.0390625, ((0, 8), (1, 16)))
    return dict(normed_input=normed_input, out_grad=out_grad, w_in=w_in, w_out=w_out)


def gelu_parts(pre):
    normal_cdf = 0.5 * (1.0 + lax.erf(pre * (1.0 / math.sqrt(2.0))))
    density = jnp.exp(-0.5 * pre * pre) * (1.0 / math.sqrt(2.0 * math.pi))
    return (pre * normal_cdf, normal_cdf + pre * density)

def reference(normed_input, out_grad, w_in, w_out):
    span = D // N_MX
    pre = jnp.zeros((TOKENS, FF), jnp.float32)
    act_grad = jnp.zeros((TOKENS, FF), jnp.float32)
    for block in range(N_MX):
        lower = block * span
        pre_part = jnp.dot(normed_input[:, lower:lower + span], w_in[lower:lower + span], preferred_element_type=jnp.float32).astype(jnp.bfloat16)
        grad_part = lax.dot_general(out_grad[:, lower:lower + span], w_out[:, lower:lower + span], (((1,), (1,)), ((), ())), preferred_element_type=jnp.float32).astype(jnp.bfloat16)
        pre_part, grad_part = lax.optimization_barrier((pre_part, grad_part))
        pre = pre + pre_part.astype(jnp.float32)
        act_grad = act_grad + grad_part.astype(jnp.float32)
    value, slope = gelu_parts(pre)
    act = value.astype(jnp.bfloat16)
    pre_grad = (act_grad * slope).astype(jnp.bfloat16)
    in_grad = lax.dot_general(pre_grad, w_in, (((1,), (1,)), ((), ())), preferred_element_type=jnp.float32).astype(jnp.bfloat16)
    total_in = jnp.zeros((D, FF), jnp.float32)
    total_out = jnp.zeros((FF, D), jnp.float32)
    for block in range(N_DP):
        lower = block * TOK_DEV
        part_in = lax.dot_general(normed_input[lower:lower + TOK_DEV], pre_grad[lower:lower + TOK_DEV], (((0,), (0,)), ((), ())), preferred_element_type=jnp.float32).astype(jnp.bfloat16)
        part_out = lax.dot_general(act[lower:lower + TOK_DEV], out_grad[lower:lower + TOK_DEV], (((0,), (0,)), ((), ())), preferred_element_type=jnp.float32).astype(jnp.bfloat16)
        part_in, part_out = lax.optimization_barrier((part_in, part_out))
        total_in = total_in + part_in.astype(jnp.float32)
        total_out = total_out + part_out.astype(jnp.float32)
    return (in_grad, total_in.astype(jnp.bfloat16), total_out.astype(jnp.bfloat16))
```

```python
import math

import jax
import jax.numpy as jnp
from jax import lax
from jax.experimental import pallas as pl
from jax.experimental.pallas import tpu as pltpu
from jax.sharding import PartitionSpec as P

MESH = pl.DeviceIdType.MESH
BF, F32 = jnp.bfloat16, jnp.float32

TOK = 1024
DC = 384
FH = 1536
SUB = 1
W = 128 * SUB
NC = FH // W
L1, L2, L3, L4, L5, L6, L7 = 1, 2, 3, 4, 5, 6, 7


def y_first(j):
    return lax.rem(j, 3) == 1


def gelu_parts(pre):
    normal_cdf = 0.5 * (1.0 + lax.erf(pre * (1.0 / math.sqrt(2.0))))
    density = jnp.exp(-0.5 * pre * pre) * (1.0 / math.sqrt(2.0 * math.pi))
    return (pre * normal_cdf, normal_cdf + pre * density)


def device(x, y, z, c):
    x, y, z = lax.rem(x + 4, 4), lax.rem(y + 4, 4), lax.rem(z + 8, 8)
    return (y // 2, x * 4 + lax.rem(y, 2) * 2 + c, z)


def position(x, y):
    x, y = lax.rem(x + 4, 4), lax.rem(y + 4, 4)
    return (y // 2) * 8 + x * 2 + lax.rem(y, 2)


def dot(a, b, ca=1, cb=0):
    return lax.dot_general(a, b, (((ca,), (cb,)), ((), ())), preferred_element_type=F32)


def wait(ref, sem):
    pltpu.make_async_copy(ref, ref, sem).wait()


def send(src, dst, ssem, rsem, to):
    pltpu.make_async_remote_copy(
        src_ref=src, dst_ref=dst, send_sem=ssem, recv_sem=rsem, device_id=to, device_id_type=MESH
    ).start()


def kernel(
    x_in, g_in, win_in, wout_in, ig_out, gwin_out, gwout_out,
    xc, xt, gc, win, wout, part, r_opp, r_left, r_right, fwd, y_buf, r_y, tile, s_in, s_out,
    ig_buf, ig_core, ig_z,
    load_sem, core_sem, core_send, w_load, w_core, w_send, rs_sem, rs_send, y_sem, y_send,
    a_sem, a_fwd, a_send, b_sem, b_fwd, b_send, dp_sem, dp_send, z_sem, z_send, xo_sem, xo_send,
    o_own, o_core, o_send, ic_sem, ic_send, iz_sem, iz_send,
):
    d, m, s = lax.axis_index("dp"), lax.axis_index("mx"), lax.axis_index("my")
    x, yl, c = m // 4, lax.rem(m // 2, 2), lax.rem(m, 2)
    y = d * 2 + yl
    core = device(x, y, s, 1 - c)
    right, left = device(x + 1, y, s, c), device(x + 3, y, s, c)
    pair = device(x, y + 1 - 2 * yl, s, c)
    across = device(x, y + 2, s, c)
    od = 1 - d
    mine = pl.ds(pl.multiple_of(c * DC, 128), DC)
    theirs = pl.ds(pl.multiple_of((1 - c) * DC, 128), DC)
    own_tok = pl.ds(pl.multiple_of(d * TOK, 128), TOK)
    other_tok = pl.ds(pl.multiple_of(od * TOK, 128), TOK)

    def hidden(core_of, j):
        return pl.ds(pl.multiple_of(core_of * FH + j * W, 128), W)

    def rows(j):
        return pl.ds(pl.multiple_of(j * W, 128), W)

    pltpu.make_async_copy(x_in, xc.at[:, mine], load_sem.at[0]).start()
    pltpu.make_async_copy(g_in, gc.at[own_tok, mine], load_sem.at[1]).start()

    @pl.loop(0, NC)
    def _(j):
        pltpu.make_async_copy(win_in.at[:, hidden(c, j)], win.at[j, mine], w_load.at[0, j]).start()
        pltpu.make_async_copy(wout_in.at[hidden(c, j)], wout.at[rows(j), mine], w_load.at[1, j]).start()

    peers = [device(x, y, s + k, c) for k in range(1, 8)]
    everyone = [core, right, left, device(x, y + 1, s, c), device(x, y + 3, s, c), across] + peers
    barrier = pltpu.get_barrier_semaphore()
    for peer in everyone:
        pl.semaphore_signal(barrier, inc=1, device_id=peer, device_id_type=MESH)
    pl.semaphore_wait(barrier, len(everyone))

    send(x_in, xc.at[:, mine], core_send.at[0], core_sem.at[0], core)
    send(g_in, gc.at[own_tok, mine], core_send.at[1], core_sem.at[1], core)

    @pl.loop(0, NC)
    def _(j):
        send(win_in.at[:, hidden(1 - c, j)], win.at[j, mine], w_send.at[0, j], w_core.at[0, j], core)
        send(wout_in.at[hidden(1 - c, j)], wout.at[rows(j), mine], w_send.at[1, j], w_core.at[1, j], core)

    wait(xc.at[:, mine], load_sem.at[0])
    wait(gc.at[own_tok, mine], load_sem.at[1])
    wait(xc.at[:, theirs], core_sem.at[0])
    wait(gc.at[own_tok, theirs], core_sem.at[1])

    nxt, prv, opp = lax.rem(x + 1, 4), lax.rem(x + 3, 4), lax.rem(x + 2, 4)

    def partial_sums(j):
        wait(win.at[j, mine], w_load.at[0, j])
        wait(wout.at[rows(j), mine], w_load.at[1, j])
        wait(win.at[j, theirs], w_core.at[0, j])
        wait(wout.at[rows(j), theirs], w_core.at[1, j])
        pre = dot(xc[...], win[j]).astype(BF)
        part[j, :, 0] = pre.reshape(8, 128, W)
        grad = dot(gc[own_tok, :], wout[rows(j), :], 1, 1).astype(BF)
        part[j, :, 1] = grad.reshape(8, 128, W)
        send(part.at[j, opp * 2], r_opp.at[j, 0], rs_send.at[0, j], rs_sem.at[0, j], right)
        send(part.at[j, opp * 2 + 1], r_opp.at[j, 1], rs_send.at[1, j], rs_sem.at[1, j], left)
        send(part.at[j, nxt * 2 + 1], r_left.at[j, 1], rs_send.at[2, j], rs_sem.at[2, j], right)
        send(part.at[j, prv * 2], r_right.at[j, 0], rs_send.at[3, j], rs_sem.at[3, j], left)

    def add_and_pass(j):
        wait(r_opp.at[j, 0], rs_sem.at[0, j])
        fwd[j, 0] = (part[j, nxt * 2].astype(F32) + r_opp[j, 0].astype(F32)).astype(BF)
        send(fwd.at[j, 0], r_left.at[j, 0], rs_send.at[4, j], rs_sem.at[4, j], right)
        wait(r_opp.at[j, 1], rs_sem.at[1, j])
        fwd[j, 1] = (part[j, prv * 2 + 1].astype(F32) + r_opp[j, 1].astype(F32)).astype(BF)
        send(fwd.at[j, 1], r_right.at[j, 1], rs_send.at[5, j], rs_sem.at[5, j], left)

    def x_sum(j, h):
        return part[j, x * 2 + h].astype(F32) + r_left[j, h].astype(F32) + r_right[j, h].astype(F32)

    def to_pair(j):
        wait(r_left.at[j, 1], rs_sem.at[2, j])
        wait(r_right.at[j, 0], rs_sem.at[3, j])
        wait(r_left.at[j, 0], rs_sem.at[4, j])
        wait(r_right.at[j, 1], rs_sem.at[5, j])
        y_buf[j] = x_sum(j, 1 - yl).astype(BF)
        send(y_buf.at[j], r_y.at[j], y_send.at[j], y_sem.at[j], pair)

    def ring(j):
        yf = y_first(j)

        def dev(da, db):
            return device(jnp.where(yf, x + db, x + da), jnp.where(yf, y + da, y + db), s, c)

        def pos(da, db):
            return position(jnp.where(yf, x + db, x + da), jnp.where(yf, y + da, y + db))

        return dev, pos

    def b_out(j, k, da):
        dev, pos = ring(j)
        ref = tile.at[j, pos(da, 0)]
        send(ref, ref, b_send.at[j], b_sem.at[0, j, k], dev(0, 1))
        send(ref, ref, b_send.at[j], b_sem.at[1, j, k], dev(0, 3))

    def activation(j):
        wait(r_y.at[j], y_sem.at[j])
        total = x_sum(j, yl) + r_y[j].astype(F32)
        value, slope = gelu_parts(total[0])
        pre_grad = (total[1] * slope).astype(BF)
        dev, pos = ring(j)
        for i in range(SUB):
            tile[j, pos(0, 0), 0, i] = value[:, i * 128 : (i + 1) * 128].T.astype(BF)
            tile[j, pos(0, 0), 1, i] = pre_grad[:, i * 128 : (i + 1) * 128]
        ref = tile.at[j, pos(0, 0)]
        send(ref, ref, a_send.at[j], a_sem.at[0, j], dev(1, 0))
        send(ref, ref, a_send.at[j], a_sem.at[1, j], dev(3, 0))
        b_out(j, 0, 0)

    def a_pass(j):
        dev, pos = ring(j)
        ref = tile.at[j, pos(3, 0)]
        wait(ref, a_sem.at[0, j])
        send(ref.at[0], ref.at[0], a_send.at[j], a_fwd.at[0, j], dev(1, 0))
        b_out(j, 1, 3)
        ref = tile.at[j, pos(1, 0)]
        wait(ref, a_sem.at[1, j])
        send(ref.at[1], ref.at[1], a_send.at[j], a_fwd.at[1, j], dev(3, 0))
        b_out(j, 2, 1)

    def a_last(j):
        dev, pos = ring(j)
        ref = tile.at[j, pos(2, 0)]
        wait(ref.at[0], a_fwd.at[0, j])
        wait(ref.at[1], a_fwd.at[1, j])
        b_out(j, 3, 2)

    order = (0, 3, 1, 2)

    def b_pass(j):
        dev, pos = ring(j)
        for k, da in enumerate(order):
            ref = tile.at[j, pos(da, 3)]
            wait(ref, b_sem.at[0, j, k])
            send(ref.at[0], ref.at[0], b_send.at[j], b_fwd.at[0, j, k], dev(0, 1))
            ref = tile.at[j, pos(da, 1)]
            wait(ref, b_sem.at[1, j, k])
            send(ref.at[1], ref.at[1], b_send.at[j], b_fwd.at[1, j, k], dev(0, 3))

    def weight_grads(j):
        dev, pos = ring(j)
        for k, da in enumerate(order):
            ref = tile.at[j, pos(da, 2)]
            wait(ref.at[0], b_fwd.at[0, j, k])
            wait(ref.at[1], b_fwd.at[1, j, k])
        for i in range(SUB):
            act = jnp.concatenate([tile[j, p, 0, i] for p in range(16)], axis=1)
            s_out[pl.ds(pl.multiple_of(j * W + i * 128, 128), 128), :] = dot(act, gc[...]).astype(BF)
        grads = [tile[j, :, 1, i].reshape(2 * TOK, 128) for i in range(SUB)]
        s_in[j] = dot(xt[...], jnp.concatenate(grads, axis=1) if SUB > 1 else grads[0]).astype(BF)
        to = gwin_out.at[:, hidden(c, j)]
        pltpu.make_async_copy(s_in.at[j, mine], to, o_own.at[0, j]).start()
        send(s_in.at[j, theirs], to, o_send.at[0, j], o_core.at[0, j], core)
        to = gwout_out.at[hidden(c, j)]
        pltpu.make_async_copy(s_out.at[rows(j), mine], to, o_own.at[1, j]).start()
        send(s_out.at[rows(j), theirs], to, o_send.at[1, j], o_core.at[1, j], core)

    def piece(of, z):
        tok = pl.ds(pl.multiple_of(of * TOK + z * 128, 128), 128)
        return xt.at[mine, tok], gc.at[tok, mine]

    def turn_inputs():
        xt[mine, own_tok] = xc[:, mine].T
        send(xt.at[mine, own_tok], xt.at[mine, own_tok], xo_send.at[0], xo_sem.at[0], core)
        for i, ref in enumerate(piece(d, s)):
            send(ref, ref, dp_send.at[i], dp_sem.at[i], across)

    def spread_inputs():
        for i, ref in enumerate(piece(od, s)):
            wait(ref, dp_sem.at[i])
            for k in range(7):
                send(ref, ref, z_send.at[i, k], z_sem.at[i, k], peers[k])

    def finish_inputs():
        for k in range(7):
            for i, ref in enumerate(piece(od, lax.rem(s + 7 - k, 8))):
                wait(ref, z_sem.at[i, k])
        send(xt.at[mine, other_tok], xt.at[mine, other_tok], xo_send.at[1], xo_sem.at[1], core)
        send(gc.at[other_tok, mine], gc.at[other_tok, mine], xo_send.at[2], xo_sem.at[2], core)

    def await_inputs():
        wait(xt.at[theirs, own_tok], xo_sem.at[0])
        wait(xt.at[theirs, other_tok], xo_sem.at[1])
        wait(gc.at[other_tok, theirs], xo_sem.at[2])

    def stage(t, lag, run):
        @pl.when((t >= lag) & (t < NC + lag))
        def _():
            run(t - lag)

    def at(t, when, run):
        pl.when(t == when)(run)

    @pl.loop(0, NC + L7)
    def _(t):
        stage(t, L1, add_and_pass)
        stage(t, L2, to_pair)
        stage(t, L3, activation)
        stage(t, 0, partial_sums)
        at(t, 0, turn_inputs)
        at(t, 2, spread_inputs)
        at(t, L7 - 1, finish_inputs)
        at(t, L7, await_inputs)
        stage(t, L4, a_pass)
        stage(t, L5, a_last)
        stage(t, L6, b_pass)
        stage(t, L7, weight_grads)

    total = None
    for j in range(NC):
        lhs = [tile[j, pl.ds(d * 8, 8), 1, i].reshape(TOK, 128) for i in range(SUB)]
        term = dot(jnp.concatenate(lhs, axis=1) if SUB > 1 else lhs[0], win[j], 1, 1)
        total = term if total is None else total + term
    total = total.astype(BF)
    ig_buf[0] = jnp.where(c == 0, total[:, :DC], total[:, DC:])
    ig_buf[1] = jnp.where(c == 0, total[:, DC:], total[:, :DC])
    send(ig_buf.at[1], ig_core, ic_send.at[0], ic_sem.at[0], core)
    wait(ig_core, ic_sem.at[0])
    ig_buf[0] = (ig_buf[0].astype(F32) + ig_core[...].astype(F32)).astype(BF)
    for k in range(7):
        to_z = lax.rem(s + k + 1, 8)
        tok = pl.ds(pl.multiple_of(to_z * 128, 128), 128)
        send(ig_buf.at[0, tok], ig_z.at[k], iz_send.at[k], iz_sem.at[k], peers[k])
    result = ig_buf[0, pl.ds(pl.multiple_of(s * 128, 128), 128), :].astype(F32)
    for k in range(7):
        wait(ig_z.at[k], iz_sem.at[k])
        result += ig_z[k].astype(F32)
    ig_out[...] = result.astype(BF)

    for i in range(2):
        wait(xc.at[:, mine], core_send.at[i])
        wait(piece(d, s)[i], dp_send.at[i])
        for k in range(7):
            wait(piece(od, s)[i], z_send.at[i, k])
    wait(xt.at[mine, own_tok], xo_send.at[0])
    wait(xt.at[mine, other_tok], xo_send.at[1])
    wait(gc.at[other_tok, mine], xo_send.at[2])
    wait(ig_buf.at[1], ic_send.at[0])
    for k in range(7):
        wait(ig_z.at[k], iz_send.at[k])

    @pl.loop(0, NC)
    def _(j):
        wait(win.at[j, mine], w_send.at[0, j])
        wait(wout.at[rows(j), mine], w_send.at[1, j])
        for i in range(6):
            wait(r_opp.at[j, 0], rs_send.at[i, j])
        wait(y_buf.at[j], y_send.at[j])
        wait(tile.at[j, pl.ds(0, 3)], a_send.at[j])
        wait(tile.at[j, pl.ds(0, 12)], b_send.at[j])
        wait(s_in.at[j, mine], o_own.at[0, j])
        wait(s_out.at[rows(j), mine], o_own.at[1, j])
        wait(s_in.at[j, theirs], o_send.at[0, j])
        wait(s_out.at[rows(j), theirs], o_send.at[1, j])
        wait(gwin_out.at[:, hidden(1 - c, j)], o_core.at[0, j])
        wait(gwout_out.at[hidden(1 - c, j)], o_core.at[1, j])


def local(normed_input, out_grad, w_in, w_out):
    any_space = pl.BlockSpec(memory_space=pl.ANY)
    dma = lambda *shape: pltpu.SemaphoreType.DMA(shape)
    vm = lambda *shape: pltpu.VMEM(shape, BF)
    return pl.pallas_call(
        kernel,
        out_shape=[
            jax.ShapeDtypeStruct((128, DC), BF),
            jax.ShapeDtypeStruct((DC, 2 * FH), BF),
            jax.ShapeDtypeStruct((2 * FH, DC), BF),
        ],
        in_specs=[any_space] * 4,
        out_specs=[pl.BlockSpec(memory_space=pltpu.VMEM), any_space, any_space],
        scratch_shapes=[
            vm(TOK, 2 * DC),
            vm(2 * DC, 2 * TOK),
            vm(2 * TOK, 2 * DC),
            vm(NC, 2 * DC, W),
            vm(FH, 2 * DC),
            vm(NC, 8, 2, 128, W),
            vm(NC, 2, 2, 128, W),
            vm(NC, 2, 2, 128, W),
            vm(NC, 2, 2, 128, W),
            vm(NC, 2, 2, 128, W),
            vm(NC, 2, 128, W),
            vm(NC, 2, 128, W),
            vm(NC, 16, 2, SUB, 128, 128),
            vm(NC, 2 * DC, W),
            vm(FH, 2 * DC),
            vm(2, TOK, DC),
            vm(TOK, DC),
            vm(7, 128, DC),
            dma(2), dma(2), dma(2),
            dma(2, NC), dma(2, NC), dma(2, NC),
            dma(6, NC), dma(6, NC), dma(NC), dma(NC),
            dma(2, NC), dma(2, NC), dma(NC),
            dma(2, NC, 4), dma(2, NC, 4), dma(NC),
            dma(2), dma(2), dma(2, 7), dma(2, 7), dma(3), dma(3),
            dma(2, NC), dma(2, NC), dma(2, NC),
            dma(1), dma(1), dma(7), dma(7),
        ],
        compiler_params=pltpu.CompilerParams(
            collective_id=0, has_side_effects=True, vmem_limit_bytes=62 << 20
        ),
        cost_estimate=pl.CostEstimate(flops=17 * 10**9, bytes_accessed=12 * 10**6, transcendentals=0),
    )(normed_input, out_grad, w_in, w_out)


def solution(mesh):
    in_specs = (P("dp", "mx"), P("dp", "mx"), P("mx", "my"), P("my", "mx"))
    out_specs = (P(("dp", "my"), "mx"), P("mx", "my"), P("my", "mx"))
    return jax.shard_map(local, mesh=mesh, in_specs=in_specs, out_specs=out_specs, check_vma=False)
```

```python
import math

import jax
import jax.numpy as jnp
from jax import lax
from jax.experimental import pallas as pl
from jax.experimental.pallas import tpu as pltpu
from jax.sharding import PartitionSpec as P

MESH = pl.DeviceIdType.MESH
BF, F32 = jnp.bfloat16, jnp.float32

TOK = 1024
DC = 384
FH = 1536
SUB = 2
W = 128 * SUB
NC = FH // W
L1, L2, L3, L4, L5, L6, L7 = 1, 2, 3, 4, 5, 6, 7
LAST = NC - 1


def y_first(j):
    return (j == 2) | (j == 3)


def gelu_parts(pre):
    normal_cdf = 0.5 * (1.0 + lax.erf(pre * (1.0 / math.sqrt(2.0))))
    density = jnp.exp(-0.5 * pre * pre) * (1.0 / math.sqrt(2.0 * math.pi))
    return (pre * normal_cdf, normal_cdf + pre * density)


def device(x, y, z, c):
    x, y, z = lax.rem(x + 4, 4), lax.rem(y + 4, 4), lax.rem(z + 8, 8)
    return (y // 2, x * 4 + lax.rem(y, 2) * 2 + c, z)


def position(x, y):
    x, y = lax.rem(x + 4, 4), lax.rem(y + 4, 4)
    return (y // 2) * 8 + x * 2 + lax.rem(y, 2)


def dot(a, b, ca=1, cb=0):
    return lax.dot_general(a, b, (((ca,), (cb,)), ((), ())), preferred_element_type=F32)


def wait(ref, sem):
    pltpu.make_async_copy(ref, ref, sem).wait()


def send(src, dst, ssem, rsem, to):
    pltpu.make_async_remote_copy(
        src_ref=src, dst_ref=dst, send_sem=ssem, recv_sem=rsem, device_id=to, device_id_type=MESH
    ).start()


def kernel(
    x_in, g_in, win_in, wout_in, ig_out, gwin_out, gwout_out,
    xc, xt, gc, win, wout, part, r_opp, r_left, r_right, fwd, y_buf, r_y, tile, s_in, s_out,
    ig_acc, ig_buf, ig_core, ig_z,
    load_sem, core_sem, core_send, w_load, w_core, w_send, rs_sem, rs_send, y_sem, y_send,
    a_sem, a_fwd, a_send, b_sem, b_fwd, b_send, dp_sem, dp_send, z_sem, z_send, xo_sem, xo_send,
    o_own, o_core, o_send, ic_sem, ic_send, iz_sem, iz_send,
):
    d, m, s = lax.axis_index("dp"), lax.axis_index("mx"), lax.axis_index("my")
    x, yl, c = m // 4, lax.rem(m // 2, 2), lax.rem(m, 2)
    y = d * 2 + yl
    core = device(x, y, s, 1 - c)
    right, left = device(x + 1, y, s, c), device(x + 3, y, s, c)
    pair = device(x, y + 1 - 2 * yl, s, c)
    across = device(x, y + 2, s, c)
    od = 1 - d
    mine = pl.ds(pl.multiple_of(c * DC, 128), DC)
    theirs = pl.ds(pl.multiple_of((1 - c) * DC, 128), DC)
    own_tok = pl.ds(pl.multiple_of(d * TOK, 128), TOK)
    other_tok = pl.ds(pl.multiple_of(od * TOK, 128), TOK)

    def hidden(core_of, j):
        return pl.ds(pl.multiple_of(core_of * FH + j * W, 128), W)

    def rows(j):
        return pl.ds(pl.multiple_of(j * W, 128), W)

    pltpu.make_async_copy(x_in, xc.at[:, mine], load_sem.at[0]).start()
    pltpu.make_async_copy(g_in, gc.at[own_tok, mine], load_sem.at[1]).start()

    @pl.loop(0, NC)
    def _(j):
        pltpu.make_async_copy(win_in.at[:, hidden(c, j)], win.at[j, mine], w_load.at[0, j]).start()
        pltpu.make_async_copy(wout_in.at[hidden(c, j)], wout.at[rows(j), mine], w_load.at[1, j]).start()

    peers = [device(x, y, s + k, c) for k in range(1, 8)]
    everyone = [core, right, left, device(x, y + 1, s, c), device(x, y + 3, s, c), across] + peers
    barrier = pltpu.get_barrier_semaphore()
    for peer in everyone:
        pl.semaphore_signal(barrier, inc=1, device_id=peer, device_id_type=MESH)
    pl.semaphore_wait(barrier, len(everyone))

    send(x_in, xc.at[:, mine], core_send.at[0], core_sem.at[0], core)
    send(g_in, gc.at[own_tok, mine], core_send.at[1], core_sem.at[1], core)

    @pl.loop(0, NC)
    def _(j):
        send(win_in.at[:, hidden(1 - c, j)], win.at[j, mine], w_send.at[0, j], w_core.at[0, j], core)
        send(wout_in.at[hidden(1 - c, j)], wout.at[rows(j), mine], w_send.at[1, j], w_core.at[1, j], core)

    wait(xc.at[:, mine], load_sem.at[0])
    wait(gc.at[own_tok, mine], load_sem.at[1])
    wait(xc.at[:, theirs], core_sem.at[0])
    wait(gc.at[own_tok, theirs], core_sem.at[1])

    nxt, prv, opp = lax.rem(x + 1, 4), lax.rem(x + 3, 4), lax.rem(x + 2, 4)

    def partial_sums(j):
        wait(win.at[j, mine], w_load.at[0, j])
        wait(wout.at[rows(j), mine], w_load.at[1, j])
        wait(win.at[j, theirs], w_core.at[0, j])
        wait(wout.at[rows(j), theirs], w_core.at[1, j])
        pre = dot(xc[...], win[j]).astype(BF)
        part[j, :, 0] = pre.reshape(8, 128, W)
        grad = dot(gc[own_tok, :], wout[rows(j), :], 1, 1).astype(BF)
        part[j, :, 1] = grad.reshape(8, 128, W)
        send(part.at[j, opp * 2], r_opp.at[j, 0], rs_send.at[0, j], rs_sem.at[0, j], right)
        send(part.at[j, opp * 2 + 1], r_opp.at[j, 1], rs_send.at[1, j], rs_sem.at[1, j], left)
        send(part.at[j, nxt * 2 + 1], r_left.at[j, 1], rs_send.at[2, j], rs_sem.at[2, j], right)
        send(part.at[j, prv * 2], r_right.at[j, 0], rs_send.at[3, j], rs_sem.at[3, j], left)

    def add_and_pass(j):
        wait(r_opp.at[j, 0], rs_sem.at[0, j])
        fwd[j, 0] = (part[j, nxt * 2].astype(F32) + r_opp[j, 0].astype(F32)).astype(BF)
        send(fwd.at[j, 0], r_left.at[j, 0], rs_send.at[4, j], rs_sem.at[4, j], right)
        wait(r_opp.at[j, 1], rs_sem.at[1, j])
        fwd[j, 1] = (part[j, prv * 2 + 1].astype(F32) + r_opp[j, 1].astype(F32)).astype(BF)
        send(fwd.at[j, 1], r_right.at[j, 1], rs_send.at[5, j], rs_sem.at[5, j], left)

    def x_sum(j, h):
        return part[j, x * 2 + h].astype(F32) + r_left[j, h].astype(F32) + r_right[j, h].astype(F32)

    def to_pair(j):
        wait(r_left.at[j, 1], rs_sem.at[2, j])
        wait(r_right.at[j, 0], rs_sem.at[3, j])
        wait(r_left.at[j, 0], rs_sem.at[4, j])
        wait(r_right.at[j, 1], rs_sem.at[5, j])
        y_buf[j] = x_sum(j, 1 - yl).astype(BF)
        send(y_buf.at[j], r_y.at[j], y_send.at[j], y_sem.at[j], pair)

    def ring(j):
        yf = y_first(j)

        def dev(da, db):
            return device(jnp.where(yf, x + db, x + da), jnp.where(yf, y + da, y + db), s, c)

        def pos(da, db):
            return position(jnp.where(yf, x + db, x + da), jnp.where(yf, y + da, y + db))

        return dev, pos

    def b_out(j, k, da):
        dev, pos = ring(j)
        ref = tile.at[j, pos(da, 0)]
        send(ref, ref, b_send.at[j], b_sem.at[0, j, k], dev(0, 1))
        send(ref, ref, b_send.at[j], b_sem.at[1, j, k], dev(0, 3))

    def activation(j):
        wait(r_y.at[j], y_sem.at[j])
        total = x_sum(j, yl) + r_y[j].astype(F32)
        value, slope = gelu_parts(total[0])
        pre_grad = (total[1] * slope).astype(BF)
        dev, pos = ring(j)
        for i in range(SUB):
            tile[j, pos(0, 0), 0, i] = value[:, i * 128 : (i + 1) * 128].T.astype(BF)
            tile[j, pos(0, 0), 1, i] = pre_grad[:, i * 128 : (i + 1) * 128]
        ref = tile.at[j, pos(0, 0)]
        send(ref, ref, a_send.at[j], a_sem.at[0, j], dev(1, 0))
        send(ref, ref, a_send.at[j], a_sem.at[1, j], dev(3, 0))
        b_out(j, 0, 0)

    def a_pass(j):
        dev, pos = ring(j)
        ref = tile.at[j, pos(3, 0)]
        wait(ref, a_sem.at[0, j])
        send(ref.at[0], ref.at[0], a_send.at[j], a_fwd.at[0, j], dev(1, 0))
        b_out(j, 1, 3)
        ref = tile.at[j, pos(1, 0)]
        wait(ref, a_sem.at[1, j])
        send(ref.at[1], ref.at[1], a_send.at[j], a_fwd.at[1, j], dev(3, 0))
        b_out(j, 2, 1)

    def a_last(j):
        dev, pos = ring(j)
        ref = tile.at[j, pos(2, 0)]
        wait(ref.at[0], a_fwd.at[0, j])
        wait(ref.at[1], a_fwd.at[1, j])
        b_out(j, 3, 2)

    order = (0, 3, 1, 2)

    PARTS = ((slice(0, 2), None),) + ((slice(0, 1), slice(1, 2)),) * 3

    def b_pass_one(j, k, which):
        dev, pos = ring(j)
        first = jnp.where(y_first(j), lax.rem(j, 2), 1 - yl)
        index = first if which == 0 else 1 - first
        place, far = jnp.where(index == 0, 3, 1), jnp.where(index == 0, 1, 3)
        ref = tile.at[j, pos(order[k], place)]
        wait(ref, b_sem.at[index, j, k])
        if PARTS[k][which] is not None:
            ref = ref.at[PARTS[k][which]]
            send(ref, ref, b_send.at[j], b_fwd.at[which, j, k], dev(0, far))

    def b_pass_half(j, which):
        for k in range(4):
            b_pass_one(j, k, which)

    def input_grad(j):
        lhs = [tile[j, pl.ds(d * 8, 8), 1, i].reshape(TOK, 128) for i in range(SUB)]
        ig_acc[...] += dot(jnp.concatenate(lhs, axis=1) if SUB > 1 else lhs[0], win[j], 1, 1)

    def b_pass(j):
        for k in range(4):
            b_pass_one(j, k, 0)
            b_pass_one(j, k, 1)

        @pl.when(jnp.logical_not(y_first(j)))
        def _():
            input_grad(j)

    def weight_grads(j):
        dev, pos = ring(j)
        for k, da in enumerate(order):
            ref = tile.at[j, pos(da, 2)]
            for which in range(2):
                if PARTS[k][which] is not None:
                    wait(ref.at[PARTS[k][which]], b_fwd.at[which, j, k])
        for i in range(SUB):
            act = jnp.concatenate([tile[j, p, 0, i] for p in range(16)], axis=1)
            s_out[pl.ds(pl.multiple_of(j * W + i * 128, 128), 128), :] = dot(act, gc[...]).astype(BF)
        grads = [tile[j, :, 1, i].reshape(2 * TOK, 128) for i in range(SUB)]
        s_in[j] = dot(xt[...], jnp.concatenate(grads, axis=1) if SUB > 1 else grads[0]).astype(BF)
        to = gwin_out.at[:, hidden(c, j)]
        pltpu.make_async_copy(s_in.at[j, mine], to, o_own.at[0, j]).start()
        send(s_in.at[j, theirs], to, o_send.at[0, j], o_core.at[0, j], core)
        to = gwout_out.at[hidden(c, j)]
        pltpu.make_async_copy(s_out.at[rows(j), mine], to, o_own.at[1, j]).start()
        send(s_out.at[rows(j), theirs], to, o_send.at[1, j], o_core.at[1, j], core)

    def weight_and_input_grads(j):
        weight_grads(j)

        @pl.when(y_first(j))
        def _():
            input_grad(j)

    def piece(of, z):
        tok = pl.ds(pl.multiple_of(of * TOK + z * 128, 128), 128)
        return xt.at[mine, tok], gc.at[tok, mine]

    def turn_inputs():
        xt[mine, own_tok] = xc[:, mine].T
        send(xt.at[mine, own_tok], xt.at[mine, own_tok], xo_send.at[0], xo_sem.at[0], core)
        for i, ref in enumerate(piece(d, s)):
            send(ref, ref, dp_send.at[i], dp_sem.at[i], across)

    def spread_inputs():
        for i, ref in enumerate(piece(od, s)):
            wait(ref, dp_sem.at[i])
            for k in range(7):
                send(ref, ref, z_send.at[i, k], z_sem.at[i, k], peers[k])

    def finish_inputs():
        for k in range(7):
            for i, ref in enumerate(piece(od, lax.rem(s + 7 - k, 8))):
                wait(ref, z_sem.at[i, k])
        send(xt.at[mine, other_tok], xt.at[mine, other_tok], xo_send.at[1], xo_sem.at[1], core)
        send(gc.at[other_tok, mine], gc.at[other_tok, mine], xo_send.at[2], xo_sem.at[2], core)

    def await_inputs():
        wait(xt.at[theirs, own_tok], xo_sem.at[0])
        wait(xt.at[theirs, other_tok], xo_sem.at[1])
        wait(gc.at[other_tok, theirs], xo_sem.at[2])

    def stage(t, lag, run, last=LAST):
        @pl.when((t >= lag) & (t <= last + lag))
        def _():
            run(t - lag)

    def at(t, when, run):
        pl.when(t == when)(run)

    ig_acc[...] = jnp.zeros_like(ig_acc)

    @pl.loop(0, LAST + L6)
    def _(t):
        stage(t, L1, add_and_pass)
        stage(t, L2, to_pair)
        stage(t, L3, activation)
        stage(t, 0, partial_sums)
        at(t, 0, turn_inputs)
        at(t, 2, spread_inputs)
        at(t, L7 - 1, finish_inputs)
        at(t, L7, await_inputs)
        stage(t, L4, a_pass)
        stage(t, L5, a_last)
        stage(t, L6, b_pass, LAST - 1)
        stage(t, L7, weight_and_input_grads, LAST - 2)

    b_pass_half(LAST, 0)
    input_grad(LAST)
    keep = ig_acc[:, mine].astype(BF)
    ig_buf[1] = ig_acc[:, theirs].astype(BF)
    send(ig_buf.at[1], ig_core, ic_send.at[0], ic_sem.at[0], core)
    b_pass_half(LAST, 1)
    wait(ig_core, ic_sem.at[0])
    ig_buf[0] = (keep.astype(F32) + ig_core[...].astype(F32)).astype(BF)
    for k in range(7):
        to_z = lax.rem(s + k + 1, 8)
        tok = pl.ds(pl.multiple_of(to_z * 128, 128), 128)
        send(ig_buf.at[0, tok], ig_z.at[k], iz_send.at[k], iz_sem.at[k], peers[k])

    @pl.loop(LAST - 1, NC)
    def _(j):
        weight_grads(j)

    result = ig_buf[0, pl.ds(pl.multiple_of(s * 128, 128), 128), :].astype(F32)
    for k in range(7):
        wait(ig_z.at[k], iz_sem.at[k])
        result += ig_z[k].astype(F32)
    ig_out[...] = result.astype(BF)

    for i in range(2):
        wait(xc.at[:, mine], core_send.at[i])
        wait(piece(d, s)[i], dp_send.at[i])
        for k in range(7):
            wait(piece(od, s)[i], z_send.at[i, k])
    wait(xt.at[mine, own_tok], xo_send.at[0])
    wait(xt.at[mine, other_tok], xo_send.at[1])
    wait(gc.at[other_tok, mine], xo_send.at[2])
    wait(ig_buf.at[1], ic_send.at[0])
    for k in range(7):
        wait(ig_z.at[k], iz_send.at[k])

    @pl.loop(0, NC)
    def _(j):
        wait(win.at[j, mine], w_send.at[0, j])
        wait(wout.at[rows(j), mine], w_send.at[1, j])
        for i in range(6):
            wait(r_opp.at[j, 0], rs_send.at[i, j])
        wait(y_buf.at[j], y_send.at[j])
        wait(tile.at[j, pl.ds(0, 3)], a_send.at[j])
        wait(tile.at[j, pl.ds(0, 12)], b_send.at[j])
        wait(s_in.at[j, mine], o_own.at[0, j])
        wait(s_out.at[rows(j), mine], o_own.at[1, j])
        wait(s_in.at[j, theirs], o_send.at[0, j])
        wait(s_out.at[rows(j), theirs], o_send.at[1, j])
        wait(gwin_out.at[:, hidden(1 - c, j)], o_core.at[0, j])
        wait(gwout_out.at[hidden(1 - c, j)], o_core.at[1, j])


def write_out(a_ref, b_ref, c_ref, a_out, b_out, c_out, sem):
    copies = [
        pltpu.make_async_copy(src, dst, sem.at[i])
        for i, (src, dst) in enumerate(((b_ref, b_out), (c_ref, c_out), (a_ref, a_out)))
    ]
    for copy in copies:
        copy.start()
    for copy in copies:
        copy.wait()


def local(normed_input, out_grad, w_in, w_out):
    any_space = pl.BlockSpec(memory_space=pl.ANY)
    dma = lambda *shape: pltpu.SemaphoreType.DMA(shape)
    vm = lambda *shape: pltpu.VMEM(shape, BF)
    shapes = [(128, DC), (DC, 2 * FH), (2 * FH, DC)]
    grads = pl.pallas_call(
        kernel,
        out_shape=[vm(*shape) for shape in shapes],
        in_specs=[any_space] * 4,
        out_specs=[pl.BlockSpec(memory_space=pltpu.VMEM)] * 3,
        scratch_shapes=[
            vm(TOK, 2 * DC),
            vm(2 * DC, 2 * TOK),
            vm(2 * TOK, 2 * DC),
            vm(NC, 2 * DC, W),
            vm(FH, 2 * DC),
            vm(NC, 8, 2, 128, W),
            vm(NC, 2, 2, 128, W),
            vm(NC, 2, 2, 128, W),
            vm(NC, 2, 2, 128, W),
            vm(NC, 2, 2, 128, W),
            vm(NC, 2, 128, W),
            vm(NC, 2, 128, W),
            vm(NC, 16, 2, SUB, 128, 128),
            vm(NC, 2 * DC, W),
            vm(FH, 2 * DC),
            pltpu.VMEM((TOK, 2 * DC), F32),
            vm(2, TOK, DC),
            vm(TOK, DC),
            vm(7, 128, DC),
            dma(2), dma(2), dma(2),
            dma(2, NC), dma(2, NC), dma(2, NC),
            dma(6, NC), dma(6, NC), dma(NC), dma(NC),
            dma(2, NC), dma(2, NC), dma(NC),
            dma(2, NC, 4), dma(2, NC, 4), dma(NC),
            dma(2), dma(2), dma(2, 7), dma(2, 7), dma(3), dma(3),
            dma(2, NC), dma(2, NC), dma(2, NC),
            dma(1), dma(1), dma(7), dma(7),
        ],
        compiler_params=pltpu.CompilerParams(
            collective_id=0, has_side_effects=True, vmem_limit_bytes=56 << 20
        ),
        cost_estimate=pl.CostEstimate(flops=17 * 10**9, bytes_accessed=12 * 10**6, transcendentals=0),
    )(normed_input, out_grad, w_in, w_out)
    return pl.pallas_call(
        write_out,
        out_shape=[jax.ShapeDtypeStruct(shape, BF) for shape in shapes],
        in_specs=[pl.BlockSpec(memory_space=pltpu.VMEM)] * 3,
        out_specs=[any_space] * 3,
        scratch_shapes=[dma(3)],
    )(*grads)


def solution(mesh):
    in_specs = (P("dp", "mx"), P("dp", "mx"), P("mx", "my"), P("my", "mx"))
    out_specs = (P(("dp", "my"), "mx"), P("mx", "my"), P("my", "mx"))
    return jax.shard_map(local, mesh=mesh, in_specs=in_specs, out_specs=out_specs, check_vma=False)
```

```python
import math

import jax
import jax.numpy as jnp
from jax import lax
from jax.experimental import pallas as pl
from jax.experimental.pallas import tpu as pltpu
from jax.sharding import PartitionSpec as P

MESH = pl.DeviceIdType.MESH
BF, F32 = jnp.bfloat16, jnp.float32

TOK = 1024
DC = 384
FH = 1536
SUB = 2
W = 128 * SUB
NC = FH // W
L1, L2, L3, L4, L5, L6, L7 = 1, 2, 3, 4, 5, 6, 7
LAST = NC - 1


def y_first(j):
    return (j == 2) | (j == 3)


def gelu_parts(pre):
    normal_cdf = 0.5 * (1.0 + lax.erf(pre * (1.0 / math.sqrt(2.0))))
    density = jnp.exp(-0.5 * pre * pre) * (1.0 / math.sqrt(2.0 * math.pi))
    return (pre * normal_cdf, normal_cdf + pre * density)


def device(x, y, z, c):
    x, y, z = lax.rem(x + 4, 4), lax.rem(y + 4, 4), lax.rem(z + 8, 8)
    return (y // 2, x * 4 + lax.rem(y, 2) * 2 + c, z)


def position(x, y):
    x, y = lax.rem(x + 4, 4), lax.rem(y + 4, 4)
    return (y // 2) * 8 + x * 2 + lax.rem(y, 2)


def dot(a, b, ca=1, cb=0):
    return lax.dot_general(a, b, (((ca,), (cb,)), ((), ())), preferred_element_type=F32)


def wait(ref, sem):
    pltpu.make_async_copy(ref, ref, sem).wait()


def send(src, dst, ssem, rsem, to):
    pltpu.make_async_remote_copy(
        src_ref=src, dst_ref=dst, send_sem=ssem, recv_sem=rsem, device_id=to, device_id_type=MESH
    ).start()


def kernel(
    x_in, g_in, win_in, wout_in, ig_out, gwin_out, gwout_out,
    xc, xt, gc, win, wout, part, r_opp, r_left, r_right, fwd, y_buf, r_y, tile, s_in, s_out,
    ig_acc, ig_buf, ig_core, ig_z,
    load_sem, core_sem, core_send, w_load, w_core, w_send, rs_sem, rs_send, y_sem, y_send,
    a_sem, a_fwd, a_send, b_sem, b_fwd, b_send, dp_sem, dp_send, z_sem, z_send, xo_sem, xo_send,
    o_own, o_core, o_send, ic_sem, ic_send, iz_sem, iz_send,
):
    d, m, s = lax.axis_index("dp"), lax.axis_index("mx"), lax.axis_index("my")
    x, yl, c = m // 4, lax.rem(m // 2, 2), lax.rem(m, 2)
    y = d * 2 + yl
    core = device(x, y, s, 1 - c)
    right, left = device(x + 1, y, s, c), device(x + 3, y, s, c)
    pair = device(x, y + 1 - 2 * yl, s, c)
    across = device(x, y + 2, s, c)
    od = 1 - d
    mine = pl.ds(pl.multiple_of(c * DC, 128), DC)
    theirs = pl.ds(pl.multiple_of((1 - c) * DC, 128), DC)
    own_tok = pl.ds(pl.multiple_of(d * TOK, 128), TOK)
    other_tok = pl.ds(pl.multiple_of(od * TOK, 128), TOK)

    def hidden(core_of, j):
        return pl.ds(pl.multiple_of(core_of * FH + j * W, 128), W)

    def rows(j):
        return pl.ds(pl.multiple_of(j * W, 128), W)

    pltpu.make_async_copy(x_in, xc.at[:, mine], load_sem.at[0]).start()
    pltpu.make_async_copy(g_in, gc.at[own_tok, mine], load_sem.at[1]).start()

    @pl.loop(0, NC)
    def _(j):
        pltpu.make_async_copy(win_in.at[:, hidden(c, j)], win.at[j, mine], w_load.at[0, j]).start()
        pltpu.make_async_copy(wout_in.at[hidden(c, j)], wout.at[rows(j), mine], w_load.at[1, j]).start()

    peers = [device(x, y, s + k, c) for k in range(1, 8)]
    everyone = [core, right, left, device(x, y + 1, s, c), device(x, y + 3, s, c), across] + peers
    barrier = pltpu.get_barrier_semaphore()
    for peer in everyone:
        pl.semaphore_signal(barrier, inc=1, device_id=peer, device_id_type=MESH)
    ig_acc[...] = jnp.zeros_like(ig_acc)
    pl.semaphore_wait(barrier, len(everyone))

    def swap_w_in(j):
        send(win_in.at[:, hidden(1 - c, j)], win.at[j, mine], w_send.at[0, j], w_core.at[0, j], core)

    def swap_w_out(j):
        send(wout_in.at[hidden(1 - c, j)], wout.at[rows(j), mine], w_send.at[1, j], w_core.at[1, j], core)

    send(x_in, xc.at[:, mine], core_send.at[0], core_sem.at[0], core)
    swap_w_in(0)
    send(g_in, gc.at[own_tok, mine], core_send.at[1], core_sem.at[1], core)
    swap_w_out(0)

    @pl.loop(1, NC)
    def _(j):
        swap_w_in(j)
        swap_w_out(j)

    wait(xc.at[:, mine], load_sem.at[0])
    wait(xc.at[:, theirs], core_sem.at[0])

    nxt, prv, opp = lax.rem(x + 1, 4), lax.rem(x + 3, 4), lax.rem(x + 2, 4)

    def partial_sums(j):
        wait(win.at[j, mine], w_load.at[0, j])
        wait(win.at[j, theirs], w_core.at[0, j])
        pre = dot(xc[...], win[j]).astype(BF)
        part[j, :, 0] = pre.reshape(8, 128, W)

        @pl.when(j == 0)
        def _():
            wait(gc.at[own_tok, mine], load_sem.at[1])
            wait(gc.at[own_tok, theirs], core_sem.at[1])

        wait(wout.at[rows(j), mine], w_load.at[1, j])
        wait(wout.at[rows(j), theirs], w_core.at[1, j])
        grad = dot(gc[own_tok, :], wout[rows(j), :], 1, 1).astype(BF)
        part[j, :, 1] = grad.reshape(8, 128, W)
        send(part.at[j, opp * 2], r_opp.at[j, 0], rs_send.at[0, j], rs_sem.at[0, j], right)
        send(part.at[j, opp * 2 + 1], r_opp.at[j, 1], rs_send.at[1, j], rs_sem.at[1, j], left)
        send(part.at[j, nxt * 2 + 1], r_left.at[j, 1], rs_send.at[2, j], rs_sem.at[2, j], right)
        send(part.at[j, prv * 2], r_right.at[j, 0], rs_send.at[3, j], rs_sem.at[3, j], left)

    def add_and_pass(j):
        wait(r_opp.at[j, 0], rs_sem.at[0, j])
        fwd[j, 0] = (part[j, nxt * 2].astype(F32) + r_opp[j, 0].astype(F32)).astype(BF)
        send(fwd.at[j, 0], r_left.at[j, 0], rs_send.at[4, j], rs_sem.at[4, j], right)
        wait(r_opp.at[j, 1], rs_sem.at[1, j])
        fwd[j, 1] = (part[j, prv * 2 + 1].astype(F32) + r_opp[j, 1].astype(F32)).astype(BF)
        send(fwd.at[j, 1], r_right.at[j, 1], rs_send.at[5, j], rs_sem.at[5, j], left)

    def x_sum(j, h):
        return part[j, x * 2 + h].astype(F32) + r_left[j, h].astype(F32) + r_right[j, h].astype(F32)

    def to_pair(j):
        wait(r_left.at[j, 1], rs_sem.at[2, j])
        wait(r_right.at[j, 0], rs_sem.at[3, j])
        wait(r_left.at[j, 0], rs_sem.at[4, j])
        wait(r_right.at[j, 1], rs_sem.at[5, j])
        y_buf[j] = x_sum(j, 1 - yl).astype(BF)
        send(y_buf.at[j], r_y.at[j], y_send.at[j], y_sem.at[j], pair)

    up, down = device(x, y + 1, s, c), device(x, y + 3, s, c)
    x_part = [lax.rem(x + i, 4) * 2 for i in range(4)]
    y_part = [(lax.rem(y + i, 4) // 2) * 8 + lax.rem(y + i, 2) for i in range(4)]

    def choose(yf, a, b):
        return tuple(jnp.where(yf, p, q) for p, q in zip(a, b))

    def ring(j):
        yf = y_first(j)
        ahead = {"a": choose(yf, up, right), "b": choose(yf, right, up)}
        behind = {"a": choose(yf, down, left), "b": choose(yf, left, down)}

        def dev(da, db):
            return (ahead if da + db == 1 else behind)["a" if da else "b"]

        def pos(da, db):
            return jnp.where(yf, x_part[db] + y_part[da], x_part[da] + y_part[db])

        return dev, pos

    def b_out(j, k, da):
        dev, pos = ring(j)
        ref = tile.at[j, pos(da, 0)]
        send(ref, ref, b_send.at[j], b_sem.at[0, j, k], dev(0, 1))
        send(ref, ref, b_send.at[j], b_sem.at[1, j, k], dev(0, 3))

    def activation(j):
        wait(r_y.at[j], y_sem.at[j])
        total = x_sum(j, yl) + r_y[j].astype(F32)
        value, slope = gelu_parts(total[0])
        pre_grad = (total[1] * slope).astype(BF)
        dev, pos = ring(j)
        for i in range(SUB):
            tile[j, pos(0, 0), 0, i] = value[:, i * 128 : (i + 1) * 128].T.astype(BF)
            tile[j, pos(0, 0), 1, i] = pre_grad[:, i * 128 : (i + 1) * 128]
        ref = tile.at[j, pos(0, 0)]
        send(ref, ref, a_send.at[j], a_sem.at[0, j], dev(1, 0))
        send(ref, ref, a_send.at[j], a_sem.at[1, j], dev(3, 0))
        b_out(j, 0, 0)

    def a_pass(j):
        dev, pos = ring(j)
        ref = tile.at[j, pos(3, 0)]
        wait(ref, a_sem.at[0, j])
        send(ref.at[0], ref.at[0], a_send.at[j], a_fwd.at[0, j], dev(1, 0))
        b_out(j, 1, 3)
        ref = tile.at[j, pos(1, 0)]
        wait(ref, a_sem.at[1, j])
        send(ref.at[1], ref.at[1], a_send.at[j], a_fwd.at[1, j], dev(3, 0))
        b_out(j, 2, 1)

    def a_last(j):
        dev, pos = ring(j)
        ref = tile.at[j, pos(2, 0)]
        wait(ref.at[0], a_fwd.at[0, j])
        wait(ref.at[1], a_fwd.at[1, j])
        b_out(j, 3, 2)

    order = (0, 3, 1, 2)

    PARTS = ((slice(0, 2), None),) + ((slice(0, 1), slice(1, 2)),) * 3

    def b_pass_one(j, k, which):
        yf = y_first(j)
        index = jnp.where(yf, lax.rem(j, 2), 1 - yl)
        index = index if which == 0 else 1 - index
        back = index == 0
        da = order[k]
        near = [jnp.where(yf, x_part[db] + y_part[da], x_part[da] + y_part[db]) for db in (3, 1)]
        ref = tile.at[j, jnp.where(back, near[0], near[1])]
        wait(ref, b_sem.at[index, j, k])
        if PARTS[k][which] is not None:
            ref = ref.at[PARTS[k][which]]
            to = choose(back, choose(yf, right, up), choose(yf, left, down))
            send(ref, ref, b_send.at[j], b_fwd.at[which, j, k], to)

    def b_pass_half(j, which):
        for k in range(4):
            b_pass_one(j, k, which)

    def input_grad(j):
        lhs = [tile[j, pl.ds(d * 8, 8), 1, i].reshape(TOK, 128) for i in range(SUB)]
        ig_acc[...] += dot(jnp.concatenate(lhs, axis=1) if SUB > 1 else lhs[0], win[j], 1, 1)

    def b_pass(j):
        for k in range(4):
            b_pass_one(j, k, 0)
            b_pass_one(j, k, 1)

        @pl.when(jnp.logical_not(y_first(j)))
        def _():
            input_grad(j)

    def weight_grads(j):
        dev, pos = ring(j)
        for k, da in enumerate(order):
            ref = tile.at[j, pos(da, 2)]
            for which in range(2):
                if PARTS[k][which] is not None:
                    wait(ref.at[PARTS[k][which]], b_fwd.at[which, j, k])
        for i in range(SUB):
            act = jnp.concatenate([tile[j, p, 0, i] for p in range(16)], axis=1)
            s_out[pl.ds(pl.multiple_of(j * W + i * 128, 128), 128), :] = dot(act, gc[...]).astype(BF)
        grads = [tile[j, :, 1, i].reshape(2 * TOK, 128) for i in range(SUB)]
        s_in[j] = dot(xt[...], jnp.concatenate(grads, axis=1) if SUB > 1 else grads[0]).astype(BF)
        to = gwin_out.at[:, hidden(c, j)]
        pltpu.make_async_copy(s_in.at[j, mine], to, o_own.at[0, j]).start()
        send(s_in.at[j, theirs], to, o_send.at[0, j], o_core.at[0, j], core)
        to = gwout_out.at[hidden(c, j)]
        pltpu.make_async_copy(s_out.at[rows(j), mine], to, o_own.at[1, j]).start()
        send(s_out.at[rows(j), theirs], to, o_send.at[1, j], o_core.at[1, j], core)

    def weight_and_input_grads(j):
        weight_grads(j)

        @pl.when(y_first(j))
        def _():
            input_grad(j)

    def piece(of, z):
        tok = pl.ds(pl.multiple_of(of * TOK + z * 128, 128), 128)
        return xt.at[mine, tok], gc.at[tok, mine]

    def turn_inputs():
        xt[mine, own_tok] = xc[:, mine].T
        send(xt.at[mine, own_tok], xt.at[mine, own_tok], xo_send.at[0], xo_sem.at[0], core)
        for i, ref in enumerate(piece(d, s)):
            send(ref, ref, dp_send.at[i], dp_sem.at[i], across)

    def spread_inputs():
        for i, ref in enumerate(piece(od, s)):
            wait(ref, dp_sem.at[i])
            for k in range(7):
                send(ref, ref, z_send.at[i, k], z_sem.at[i, k], peers[k])

    def finish_inputs():
        for k in range(7):
            for i, ref in enumerate(piece(od, lax.rem(s + 7 - k, 8))):
                wait(ref, z_sem.at[i, k])
        send(xt.at[mine, other_tok], xt.at[mine, other_tok], xo_send.at[1], xo_sem.at[1], core)
        send(gc.at[other_tok, mine], gc.at[other_tok, mine], xo_send.at[2], xo_sem.at[2], core)

    def await_inputs():
        wait(xt.at[theirs, own_tok], xo_sem.at[0])
        wait(xt.at[theirs, other_tok], xo_sem.at[1])
        wait(gc.at[other_tok, theirs], xo_sem.at[2])

    def stage(t, lag, run, last=LAST):
        @pl.when((t >= lag) & (t <= last + lag))
        def _():
            run(t - lag)

    def at(t, when, run):
        pl.when(t == when)(run)

    @pl.loop(0, LAST + L6)
    def _(t):
        stage(t, L4, a_pass)
        stage(t, L3, activation)
        stage(t, L5, a_last)
        stage(t, L2, to_pair)
        stage(t, L1, add_and_pass)
        stage(t, 0, partial_sums)
        at(t, 0, turn_inputs)
        at(t, 1, spread_inputs)
        at(t, L7 - 1, finish_inputs)
        at(t, L7, await_inputs)
        stage(t, L6, b_pass, LAST - 1)
        stage(t, L7, weight_and_input_grads, LAST + L6 - 1 - L7)

    def z_step(n):
        for way, to in enumerate((peers[0], peers[6])):
            start = lax.rem(s + (4 - n if way == 0 else 4 + n), 8) * 128
            half = pl.ds(pl.multiple_of(start + way * 64, 64), 64)
            block = pl.ds(pl.multiple_of(start, 128), 128)
            if n == 0:
                send(ig_buf.at[0, half], ig_z.at[way, 0, pl.ds(0, 64)], iz_send.at[way, 0], iz_sem.at[way, 0], to)
                continue
            came = ig_z.at[way, 0, pl.ds(0, 64)] if n == 1 else ig_z.at[way, n - 1]
            rows_in = half if n == 1 else block
            wait(came, iz_sem.at[way, n - 1])
            ig_buf[0, rows_in] = (ig_buf[0, rows_in].astype(F32) + came[...].astype(F32)).astype(BF)
            send(ig_buf.at[0, block], ig_z.at[way, n], iz_send.at[way, n], iz_sem.at[way, n], to)

    b_pass_half(LAST, 0)
    input_grad(LAST)
    keep = ig_acc[:, mine].astype(BF)
    ig_buf[1] = ig_acc[:, theirs].astype(BF)
    send(ig_buf.at[1], ig_core, ic_send.at[0], ic_sem.at[0], core)
    wait(ig_core, ic_sem.at[0])
    ig_buf[0] = (keep.astype(F32) + ig_core[...].astype(F32)).astype(BF)
    z_step(0)
    b_pass_half(LAST, 1)
    z_step(1)
    weight_grads(LAST - 1)
    z_step(2)
    z_step(3)
    weight_grads(LAST)
    result = ig_buf[0, pl.ds(pl.multiple_of(s * 128, 128), 128), :].astype(F32)
    for way in range(2):
        wait(ig_z.at[way, 3], iz_sem.at[way, 3])
        result += ig_z[way, 3].astype(F32)
    ig_out[...] = result.astype(BF)

    for i in range(2):
        wait(xc.at[:, mine], core_send.at[i])
        wait(piece(d, s)[i], dp_send.at[i])
        for k in range(7):
            wait(piece(od, s)[i], z_send.at[i, k])
    wait(xt.at[mine, own_tok], xo_send.at[0])
    wait(xt.at[mine, other_tok], xo_send.at[1])
    wait(gc.at[other_tok, mine], xo_send.at[2])
    wait(ig_buf.at[1], ic_send.at[0])
    for way in range(2):
        wait(ig_z.at[way, 0, pl.ds(0, 64)], iz_send.at[way, 0])
        for n in range(1, 4):
            wait(ig_z.at[way, n], iz_send.at[way, n])

    @pl.loop(0, NC)
    def _(j):
        wait(win.at[j, mine], w_send.at[0, j])
        wait(wout.at[rows(j), mine], w_send.at[1, j])
        for i in range(6):
            wait(r_opp.at[j, 0], rs_send.at[i, j])
        wait(y_buf.at[j], y_send.at[j])
        wait(tile.at[j, pl.ds(0, 3)], a_send.at[j])
        wait(tile.at[j, pl.ds(0, 12)], b_send.at[j])
        wait(s_in.at[j, mine], o_own.at[0, j])
        wait(s_out.at[rows(j), mine], o_own.at[1, j])
        wait(s_in.at[j, theirs], o_send.at[0, j])
        wait(s_out.at[rows(j), theirs], o_send.at[1, j])
        wait(gwin_out.at[:, hidden(1 - c, j)], o_core.at[0, j])
        wait(gwout_out.at[hidden(1 - c, j)], o_core.at[1, j])


def write_out(a_ref, b_ref, c_ref, a_out, b_out, c_out, sem):
    copies = [
        pltpu.make_async_copy(src, dst, sem.at[i])
        for i, (src, dst) in enumerate(((b_ref, b_out), (c_ref, c_out), (a_ref, a_out)))
    ]
    for copy in copies:
        copy.start()
    for copy in copies:
        copy.wait()


def local(normed_input, out_grad, w_in, w_out):
    any_space = pl.BlockSpec(memory_space=pl.ANY)
    dma = lambda *shape: pltpu.SemaphoreType.DMA(shape)
    vm = lambda *shape: pltpu.VMEM(shape, BF)
    shapes = [(128, DC), (DC, 2 * FH), (2 * FH, DC)]
    grads = pl.pallas_call(
        kernel,
        out_shape=[vm(*shape) for shape in shapes],
        in_specs=[any_space] * 4,
        out_specs=[pl.BlockSpec(memory_space=pltpu.VMEM)] * 3,
        scratch_shapes=[
            vm(TOK, 2 * DC),
            vm(2 * DC, 2 * TOK),
            vm(2 * TOK, 2 * DC),
            vm(NC, 2 * DC, W),
            vm(FH, 2 * DC),
            vm(NC, 8, 2, 128, W),
            vm(NC, 2, 2, 128, W),
            vm(NC, 2, 2, 128, W),
            vm(NC, 2, 2, 128, W),
            vm(NC, 2, 2, 128, W),
            vm(NC, 2, 128, W),
            vm(NC, 2, 128, W),
            vm(NC, 16, 2, SUB, 128, 128),
            vm(NC, 2 * DC, W),
            vm(FH, 2 * DC),
            pltpu.VMEM((TOK, 2 * DC), F32),
            vm(2, TOK, DC),
            vm(TOK, DC),
            vm(2, 4, 128, DC),
            dma(2), dma(2), dma(2),
            dma(2, NC), dma(2, NC), dma(2, NC),
            dma(6, NC), dma(6, NC), dma(NC), dma(NC),
            dma(2, NC), dma(2, NC), dma(NC),
            dma(2, NC, 4), dma(2, NC, 4), dma(NC),
            dma(2), dma(2), dma(2, 7), dma(2, 7), dma(3), dma(3),
            dma(2, NC), dma(2, NC), dma(2, NC),
            dma(1), dma(1), dma(2, 4), dma(2, 4),
        ],
        compiler_params=pltpu.CompilerParams(
            collective_id=0, has_side_effects=True, vmem_limit_bytes=56 << 20
        ),
        cost_estimate=pl.CostEstimate(flops=17 * 10**9, bytes_accessed=12 * 10**6, transcendentals=0),
    )(normed_input, out_grad, w_in, w_out)
    return pl.pallas_call(
        write_out,
        out_shape=[jax.ShapeDtypeStruct(shape, BF) for shape in shapes],
        in_specs=[pl.BlockSpec(memory_space=pltpu.VMEM)] * 3,
        out_specs=[any_space] * 3,
        scratch_shapes=[dma(3)],
    )(*grads)


def solution(mesh):
    in_specs = (P("dp", "mx"), P("dp", "mx"), P("mx", "my"), P("my", "mx"))
    out_specs = (P(("dp", "my"), "mx"), P("mx", "my"), P("my", "mx"))
    return jax.shard_map(local, mesh=mesh, in_specs=in_specs, out_specs=out_specs, check_vma=False)
```

```python
import math

import jax
import jax.numpy as jnp
from jax import lax
from jax.experimental import pallas as pl
from jax.experimental.pallas import tpu as pltpu
from jax.sharding import PartitionSpec as P

MESH = pl.DeviceIdType.MESH
BF, F32 = jnp.bfloat16, jnp.float32

TOK = 1024
DC = 384
FH = 1536
SUB = 2
W = 128 * SUB
NC = FH // W
L1, L2, L3, L4, L5, L6, L7 = 1, 2, 3, 4, 5, 6, 7
LAST = NC - 1


def y_first(j):
    return (j == 2) | (j == 3)


def gelu_parts(pre):
    normal_cdf = 0.5 * (1.0 + lax.erf(pre * (1.0 / math.sqrt(2.0))))
    density = jnp.exp(-0.5 * pre * pre) * (1.0 / math.sqrt(2.0 * math.pi))
    return (pre * normal_cdf, normal_cdf + pre * density)


def device(x, y, z, c):
    x, y, z = lax.rem(x + 4, 4), lax.rem(y + 4, 4), lax.rem(z + 8, 8)
    return (y // 2, x * 4 + lax.rem(y, 2) * 2 + c, z)


def position(x, y):
    x, y = lax.rem(x + 4, 4), lax.rem(y + 4, 4)
    return (y // 2) * 8 + x * 2 + lax.rem(y, 2)


def dot(a, b, ca=1, cb=0):
    return lax.dot_general(a, b, (((ca,), (cb,)), ((), ())), preferred_element_type=F32)


def wait(ref, sem):
    pltpu.make_async_copy(ref, ref, sem).wait()


def send(src, dst, ssem, rsem, to):
    pltpu.make_async_remote_copy(
        src_ref=src, dst_ref=dst, send_sem=ssem, recv_sem=rsem, device_id=to, device_id_type=MESH
    ).start()


def kernel(
    x_in, g_in, win_in, wout_in, ig_out, gwin_out, gwout_out,
    xc, xt, gc, win, wout, part, r_opp, r_left, r_right, fwd, y_buf, r_y, tile, s_in, s_out,
    ig_acc, ig_buf, ig_core, ig_z,
    load_sem, core_sem, core_send, w_load, w_core, w_send, rs_sem, rs_send, y_sem, y_send,
    a_sem, a_fwd, a_send, b_sem, b_fwd, b_send, dp_sem, dp_send, z_sem, z_send, xo_sem, xo_send,
    o_own, o_core, o_send, ic_sem, ic_send, iz_sem, iz_send,
):
    d, m, s = lax.axis_index("dp"), lax.axis_index("mx"), lax.axis_index("my")
    x, yl, c = m // 4, lax.rem(m // 2, 2), lax.rem(m, 2)
    y = d * 2 + yl
    core = device(x, y, s, 1 - c)
    right, left = device(x + 1, y, s, c), device(x + 3, y, s, c)
    pair = device(x, y + 1 - 2 * yl, s, c)
    across = device(x, y + 2, s, c)
    od = 1 - d
    mine = pl.ds(pl.multiple_of(c * DC, 128), DC)
    theirs = pl.ds(pl.multiple_of((1 - c) * DC, 128), DC)
    own_tok = pl.ds(pl.multiple_of(d * TOK, 128), TOK)
    other_tok = pl.ds(pl.multiple_of(od * TOK, 128), TOK)

    def hidden(core_of, j):
        return pl.ds(pl.multiple_of(core_of * FH + j * W, 128), W)

    def rows(j):
        return pl.ds(pl.multiple_of(j * W, 128), W)

    pltpu.make_async_copy(x_in, xc.at[:, mine], load_sem.at[0]).start()
    pltpu.make_async_copy(g_in, gc.at[own_tok, mine], load_sem.at[1]).start()

    @pl.loop(0, NC)
    def _(j):
        pltpu.make_async_copy(win_in.at[:, hidden(c, j)], win.at[j, mine], w_load.at[0, j]).start()
        pltpu.make_async_copy(wout_in.at[hidden(c, j)], wout.at[rows(j), mine], w_load.at[1, j]).start()

    peers = [device(x, y, s + k, c) for k in range(1, 8)]
    everyone = [core, right, left, device(x, y + 1, s, c), device(x, y + 3, s, c), across] + peers
    barrier = pltpu.get_barrier_semaphore()
    for peer in everyone:
        pl.semaphore_signal(barrier, inc=1, device_id=peer, device_id_type=MESH)
    ig_acc[...] = jnp.zeros_like(ig_acc)
    pl.semaphore_wait(barrier, len(everyone))

    def swap_w_in(j):
        send(win_in.at[:, hidden(1 - c, j)], win.at[j, mine], w_send.at[0, j], w_core.at[0, j], core)

    def swap_w_out(j):
        send(wout_in.at[hidden(1 - c, j)], wout.at[rows(j), mine], w_send.at[1, j], w_core.at[1, j], core)

    send(x_in, xc.at[:, mine], core_send.at[0], core_sem.at[0], core)
    swap_w_in(0)
    send(g_in, gc.at[own_tok, mine], core_send.at[1], core_sem.at[1], core)
    swap_w_out(0)

    @pl.loop(1, NC)
    def _(j):
        swap_w_in(j)
        swap_w_out(j)

    wait(xc.at[:, mine], load_sem.at[0])
    wait(xc.at[:, theirs], core_sem.at[0])

    nxt, prv, opp = lax.rem(x + 1, 4), lax.rem(x + 3, 4), lax.rem(x + 2, 4)

    def partial_sums(j):
        wait(win.at[j, mine], w_load.at[0, j])
        wait(win.at[j, theirs], w_core.at[0, j])
        pre = dot(xc[...], win[j]).astype(BF)
        part[j, :, 0] = pre.reshape(8, 128, W)

        @pl.when(j == 0)
        def _():
            wait(gc.at[own_tok, mine], load_sem.at[1])
            wait(gc.at[own_tok, theirs], core_sem.at[1])

        wait(wout.at[rows(j), mine], w_load.at[1, j])
        wait(wout.at[rows(j), theirs], w_core.at[1, j])
        grad = dot(gc[own_tok, :], wout[rows(j), :], 1, 1).astype(BF)
        part[j, :, 1] = grad.reshape(8, 128, W)
        send(part.at[j, opp * 2], r_opp.at[j, 0], rs_send.at[0, j], rs_sem.at[0, j], right)
        send(part.at[j, opp * 2 + 1], r_opp.at[j, 1], rs_send.at[1, j], rs_sem.at[1, j], left)
        send(part.at[j, nxt * 2 + 1], r_left.at[j, 1], rs_send.at[2, j], rs_sem.at[2, j], right)
        send(part.at[j, prv * 2], r_right.at[j, 0], rs_send.at[3, j], rs_sem.at[3, j], left)

    def add_and_pass(j):
        wait(r_opp.at[j, 0], rs_sem.at[0, j])
        fwd[j, 0] = (part[j, nxt * 2].astype(F32) + r_opp[j, 0].astype(F32)).astype(BF)
        send(fwd.at[j, 0], r_left.at[j, 0], rs_send.at[4, j], rs_sem.at[4, j], right)
        wait(r_opp.at[j, 1], rs_sem.at[1, j])
        fwd[j, 1] = (part[j, prv * 2 + 1].astype(F32) + r_opp[j, 1].astype(F32)).astype(BF)
        send(fwd.at[j, 1], r_right.at[j, 1], rs_send.at[5, j], rs_sem.at[5, j], left)

    def x_sum(j, h):
        return part[j, x * 2 + h].astype(F32) + r_left[j, h].astype(F32) + r_right[j, h].astype(F32)

    def to_pair(j):
        wait(r_left.at[j, 1], rs_sem.at[2, j])
        wait(r_right.at[j, 0], rs_sem.at[3, j])
        wait(r_left.at[j, 0], rs_sem.at[4, j])
        wait(r_right.at[j, 1], rs_sem.at[5, j])
        y_buf[j] = x_sum(j, 1 - yl).astype(BF)
        send(y_buf.at[j], r_y.at[j], y_send.at[j], y_sem.at[j], pair)

    up, down = device(x, y + 1, s, c), device(x, y + 3, s, c)
    x_part = [lax.rem(x + i, 4) * 2 for i in range(4)]
    y_part = [(lax.rem(y + i, 4) // 2) * 8 + lax.rem(y + i, 2) for i in range(4)]

    def choose(yf, a, b):
        return tuple(jnp.where(yf, p, q) for p, q in zip(a, b))

    def ring(j):
        yf = y_first(j)
        ahead = {"a": choose(yf, up, right), "b": choose(yf, right, up)}
        behind = {"a": choose(yf, down, left), "b": choose(yf, left, down)}

        def dev(da, db):
            return (ahead if da + db == 1 else behind)["a" if da else "b"]

        def pos(da, db):
            return jnp.where(yf, x_part[db] + y_part[da], x_part[da] + y_part[db])

        return dev, pos

    def b_out(j, k, da):
        dev, pos = ring(j)
        ref = tile.at[j, pos(da, 0)]
        send(ref, ref, b_send.at[j], b_sem.at[0, j, k], dev(0, 1))
        send(ref, ref, b_send.at[j], b_sem.at[1, j, k], dev(0, 3))

    def activation(j):
        wait(r_y.at[j], y_sem.at[j])
        total = x_sum(j, yl) + r_y[j].astype(F32)
        value, slope = gelu_parts(total[0])
        pre_grad = (total[1] * slope).astype(BF)
        dev, pos = ring(j)
        for i in range(SUB):
            tile[j, pos(0, 0), 0, i] = value[:, i * 128 : (i + 1) * 128].T.astype(BF)
            tile[j, pos(0, 0), 1, i] = pre_grad[:, i * 128 : (i + 1) * 128]
        ref = tile.at[j, pos(0, 0)]
        send(ref, ref, a_send.at[j], a_sem.at[0, j], dev(1, 0))
        send(ref, ref, a_send.at[j], a_sem.at[1, j], dev(3, 0))
        b_out(j, 0, 0)

    def a_pass(j):
        dev, pos = ring(j)
        ref = tile.at[j, pos(3, 0)]
        wait(ref, a_sem.at[0, j])
        send(ref.at[0], ref.at[0], a_send.at[j], a_fwd.at[0, j], dev(1, 0))
        b_out(j, 1, 3)
        ref = tile.at[j, pos(1, 0)]
        wait(ref, a_sem.at[1, j])
        send(ref.at[1], ref.at[1], a_send.at[j], a_fwd.at[1, j], dev(3, 0))
        b_out(j, 2, 1)

    def a_last(j):
        dev, pos = ring(j)
        ref = tile.at[j, pos(2, 0)]
        wait(ref.at[0], a_fwd.at[0, j])
        wait(ref.at[1], a_fwd.at[1, j])
        b_out(j, 3, 2)

    order = (0, 3, 1, 2)

    PARTS = ((slice(0, 2), None),) + ((slice(0, 1), slice(1, 2)),) * 3

    def b_pass_one(j, k, which):
        yf = y_first(j)
        index = jnp.where(yf, lax.rem(j, 2), 1 - yl)
        index = index if which == 0 else 1 - index
        back = index == 0
        da = order[k]
        near = [jnp.where(yf, x_part[db] + y_part[da], x_part[da] + y_part[db]) for db in (3, 1)]
        ref = tile.at[j, jnp.where(back, near[0], near[1])]
        wait(ref, b_sem.at[index, j, k])
        if PARTS[k][which] is not None:
            ref = ref.at[PARTS[k][which]]
            to = choose(back, choose(yf, right, up), choose(yf, left, down))
            send(ref, ref, b_send.at[j], b_fwd.at[which, j, k], to)

    def b_pass_half(j, which):
        for k in range(4):
            b_pass_one(j, k, which)

    def input_grad(j):
        lhs = [tile[j, pl.ds(d * 8, 8), 1, i].reshape(TOK, 128) for i in range(SUB)]
        ig_acc[...] += dot(jnp.concatenate(lhs, axis=1) if SUB > 1 else lhs[0], win[j], 1, 1)

    def b_pass(j):
        for k in range(4):
            b_pass_one(j, k, 0)
            b_pass_one(j, k, 1)

        @pl.when(jnp.logical_not(y_first(j)))
        def _():
            input_grad(j)

    def weight_grads(j):
        dev, pos = ring(j)
        for k, da in enumerate(order):
            ref = tile.at[j, pos(da, 2)]
            for which in range(2):
                if PARTS[k][which] is not None:
                    wait(ref.at[PARTS[k][which]], b_fwd.at[which, j, k])
        for i in range(SUB):
            act = jnp.concatenate([tile[j, p, 0, i] for p in range(16)], axis=1)
            s_out[pl.ds(pl.multiple_of(j * W + i * 128, 128), 128), :] = dot(act, gc[...]).astype(BF)
        to = gwout_out.at[hidden(c, j)]
        pltpu.make_async_copy(s_out.at[rows(j), mine], to, o_own.at[1, j]).start()
        send(s_out.at[rows(j), theirs], to, o_send.at[1, j], o_core.at[1, j], core)
        grads = [tile[j, :, 1, i].reshape(2 * TOK, 128) for i in range(SUB)]
        s_in[j] = dot(xt[...], jnp.concatenate(grads, axis=1) if SUB > 1 else grads[0]).astype(BF)
        to = gwin_out.at[:, hidden(c, j)]
        pltpu.make_async_copy(s_in.at[j, mine], to, o_own.at[0, j]).start()
        send(s_in.at[j, theirs], to, o_send.at[0, j], o_core.at[0, j], core)

    def weight_and_input_grads(j):
        weight_grads(j)

        @pl.when(y_first(j))
        def _():
            input_grad(j)

    def piece(of, z):
        tok = pl.ds(pl.multiple_of(of * TOK + z * 128, 128), 128)
        return xt.at[mine, tok], gc.at[tok, mine]

    def turn_inputs():
        xt[mine, own_tok] = xc[:, mine].T
        send(xt.at[mine, own_tok], xt.at[mine, own_tok], xo_send.at[0], xo_sem.at[0], core)
        for i, ref in enumerate(piece(d, s)):
            send(ref, ref, dp_send.at[i], dp_sem.at[i], across)

    def spread_inputs():
        for i, ref in enumerate(piece(od, s)):
            wait(ref, dp_sem.at[i])
            for k in range(7):
                send(ref, ref, z_send.at[i, k], z_sem.at[i, k], peers[k])

    def finish_inputs():
        for k in range(7):
            for i, ref in enumerate(piece(od, lax.rem(s + 7 - k, 8))):
                wait(ref, z_sem.at[i, k])
        send(xt.at[mine, other_tok], xt.at[mine, other_tok], xo_send.at[1], xo_sem.at[1], core)
        send(gc.at[other_tok, mine], gc.at[other_tok, mine], xo_send.at[2], xo_sem.at[2], core)

    def await_inputs():
        wait(xt.at[theirs, own_tok], xo_sem.at[0])
        wait(xt.at[theirs, other_tok], xo_sem.at[1])
        wait(gc.at[other_tok, theirs], xo_sem.at[2])

    def stage(t, lag, run, last=LAST):
        @pl.when((t >= lag) & (t <= last + lag))
        def _():
            run(t - lag)

    def at(t, when, run):
        pl.when(t == when)(run)

    @pl.loop(0, LAST + L6)
    def _(t):
        stage(t, L4, a_pass)
        stage(t, L3, activation)
        stage(t, L5, a_last)
        stage(t, L2, to_pair)
        stage(t, L1, add_and_pass)
        stage(t, 0, partial_sums)
        at(t, 0, turn_inputs)
        at(t, 1, spread_inputs)
        at(t, L7 - 1, finish_inputs)
        at(t, L7, await_inputs)
        stage(t, L6, b_pass, LAST - 1)
        stage(t, L7, weight_and_input_grads, LAST + L6 - 1 - L7)

    def z_step(n):
        for way, to in enumerate((peers[0], peers[6])):
            start = lax.rem(s + (4 - n if way == 0 else 4 + n), 8) * 128
            half = pl.ds(pl.multiple_of(start + way * 64, 64), 64)
            block = pl.ds(pl.multiple_of(start, 128), 128)
            if n == 0:
                send(ig_buf.at[0, half], ig_z.at[way, 0, pl.ds(0, 64)], iz_send.at[way, 0], iz_sem.at[way, 0], to)
                continue
            came = ig_z.at[way, 0, pl.ds(0, 64)] if n == 1 else ig_z.at[way, n - 1]
            rows_in = half if n == 1 else block
            wait(came, iz_sem.at[way, n - 1])
            ig_buf[0, rows_in] = (ig_buf[0, rows_in].astype(F32) + came[...].astype(F32)).astype(BF)
            send(ig_buf.at[0, block], ig_z.at[way, n], iz_send.at[way, n], iz_sem.at[way, n], to)

    b_pass_half(LAST, 0)
    input_grad(LAST)
    keep = ig_acc[:, mine].astype(BF)
    ig_buf[1] = ig_acc[:, theirs].astype(BF)
    send(ig_buf.at[1], ig_core, ic_send.at[0], ic_sem.at[0], core)
    wait(ig_core, ic_sem.at[0])
    ig_buf[0] = (keep.astype(F32) + ig_core[...].astype(F32)).astype(BF)
    z_step(0)
    b_pass_half(LAST, 1)
    z_step(1)
    weight_grads(LAST - 1)
    z_step(2)
    z_step(3)
    weight_grads(LAST)
    result = ig_buf[0, pl.ds(pl.multiple_of(s * 128, 128), 128), :].astype(F32)
    for way in range(2):
        wait(ig_z.at[way, 3], iz_sem.at[way, 3])
        result += ig_z[way, 3].astype(F32)
    ig_out[...] = result.astype(BF)

    for i in range(2):
        wait(xc.at[:, mine], core_send.at[i])
        wait(piece(d, s)[i], dp_send.at[i])
        for k in range(7):
            wait(piece(od, s)[i], z_send.at[i, k])
    wait(xt.at[mine, own_tok], xo_send.at[0])
    wait(xt.at[mine, other_tok], xo_send.at[1])
    wait(gc.at[other_tok, mine], xo_send.at[2])
    wait(ig_buf.at[1], ic_send.at[0])
    for way in range(2):
        wait(ig_z.at[way, 0, pl.ds(0, 64)], iz_send.at[way, 0])
        for n in range(1, 4):
            wait(ig_z.at[way, n], iz_send.at[way, n])

    @pl.loop(0, NC)
    def _(j):
        wait(win.at[j, mine], w_send.at[0, j])
        wait(wout.at[rows(j), mine], w_send.at[1, j])
        for i in range(6):
            wait(r_opp.at[j, 0], rs_send.at[i, j])
        wait(y_buf.at[j], y_send.at[j])
        wait(tile.at[j, pl.ds(0, 3)], a_send.at[j])
        wait(tile.at[j, pl.ds(0, 12)], b_send.at[j])
        wait(s_in.at[j, mine], o_own.at[0, j])
        wait(s_out.at[rows(j), mine], o_own.at[1, j])
        wait(s_in.at[j, theirs], o_send.at[0, j])
        wait(s_out.at[rows(j), theirs], o_send.at[1, j])
        wait(gwin_out.at[:, hidden(1 - c, j)], o_core.at[0, j])
        wait(gwout_out.at[hidden(1 - c, j)], o_core.at[1, j])


def write_out(a_ref, b_ref, c_ref, a_out, b_out, c_out, sem):
    copies = [
        pltpu.make_async_copy(src, dst, sem.at[i])
        for i, (src, dst) in enumerate(((b_ref, b_out), (c_ref, c_out), (a_ref, a_out)))
    ]
    for copy in copies:
        copy.start()
    for copy in copies:
        copy.wait()


def local(normed_input, out_grad, w_in, w_out):
    any_space = pl.BlockSpec(memory_space=pl.ANY)
    dma = lambda *shape: pltpu.SemaphoreType.DMA(shape)
    vm = lambda *shape: pltpu.VMEM(shape, BF)
    shapes = [(128, DC), (DC, 2 * FH), (2 * FH, DC)]
    grads = pl.pallas_call(
        kernel,
        out_shape=[vm(*shape) for shape in shapes],
        in_specs=[any_space] * 4,
        out_specs=[pl.BlockSpec(memory_space=pltpu.VMEM)] * 3,
        scratch_shapes=[
            vm(TOK, 2 * DC),
            vm(2 * DC, 2 * TOK),
            vm(2 * TOK, 2 * DC),
            vm(NC, 2 * DC, W),
            vm(FH, 2 * DC),
            vm(NC, 8, 2, 128, W),
            vm(NC, 2, 2, 128, W),
            vm(NC, 2, 2, 128, W),
            vm(NC, 2, 2, 128, W),
            vm(NC, 2, 2, 128, W),
            vm(NC, 2, 128, W),
            vm(NC, 2, 128, W),
            vm(NC, 16, 2, SUB, 128, 128),
            vm(NC, 2 * DC, W),
            vm(FH, 2 * DC),
            pltpu.VMEM((TOK, 2 * DC), F32),
            vm(2, TOK, DC),
            vm(TOK, DC),
            vm(2, 4, 128, DC),
            dma(2), dma(2), dma(2),
            dma(2, NC), dma(2, NC), dma(2, NC),
            dma(6, NC), dma(6, NC), dma(NC), dma(NC),
            dma(2, NC), dma(2, NC), dma(NC),
            dma(2, NC, 4), dma(2, NC, 4), dma(NC),
            dma(2), dma(2), dma(2, 7), dma(2, 7), dma(3), dma(3),
            dma(2, NC), dma(2, NC), dma(2, NC),
            dma(1), dma(1), dma(2, 4), dma(2, 4),
        ],
        compiler_params=pltpu.CompilerParams(
            collective_id=0, has_side_effects=True, vmem_limit_bytes=56 << 20
        ),
        cost_estimate=pl.CostEstimate(flops=17 * 10**9, bytes_accessed=12 * 10**6, transcendentals=0),
    )(normed_input, out_grad, w_in, w_out)
    return pl.pallas_call(
        write_out,
        out_shape=[jax.ShapeDtypeStruct(shape, BF) for shape in shapes],
        in_specs=[pl.BlockSpec(memory_space=pltpu.VMEM)] * 3,
        out_specs=[any_space] * 3,
        scratch_shapes=[dma(3)],
    )(*grads)


def solution(mesh):
    in_specs = (P("dp", "mx"), P("dp", "mx"), P("mx", "my"), P("my", "mx"))
    out_specs = (P(("dp", "my"), "mx"), P("mx", "my"), P("my", "mx"))
    return jax.shard_map(local, mesh=mesh, in_specs=in_specs, out_specs=out_specs, check_vma=False)
```
